128 devices in a mesh: dp: 16 (over y, x), tensor: 8 (over z, core).
Axes of the slice: x: 4, y: 4, z: 4, core: 2. Of those that a mesh axis runs over, the one named last changes fastest.
Arguments:
- queries: bfloat16 [256, 64, 8192], P('dp', None, 'tensor'), may hold values from -10 to 50
- fresh_kv: bfloat16 [256, 2, 64, 1024], P('dp', None, None, 'tensor'), may hold values from -6 to 7.5
- kv_cache: bfloat16 [256, 2, 512, 1024], P('dp', None, None, 'tensor'), may hold values from -6 to 7.5
- parent_device: int32 [256, 1], P('dp'), may hold values from 0 to 15; in each aligned block of 16 rows (0 to 15, 16 to 31, ...) at most 2 rows name the same one
- parent_rank: int32 [256], P('dp'), may hold values from 0 to 1
- cache_length: int32 [8], replicated, may hold values from 1 to 512, 2560 in all
- out_weight: bfloat16 [8192, 8192], P('tensor'), may hold values from -1 to 1
- residual: bfloat16 [256, 64, 8192], P('dp', None, 'tensor'), may hold values from -132 to 132
- norm_gain: bfloat16 [8192], P('tensor'), may hold values from 0.25 to 1.75
Outputs:
- normed: bfloat16 [256, 64, 8192], P('dp', None, 'tensor')
The draws below stay inside these ranges and needn't reach their ends.
Inputs may be any that keep to these rules, and one draw needn't show every extreme that they name: `parent_device`: among the 16 beams of one dp index, at most 2 have their parent on the same dp index, and in every draw some dp index has exactly 2 parents on one dp index. `cache_length`: some problem has exactly 512 live positions in every draw.
All inputs are finite; a program needn't handle non-finite values.
Results may differ from the reference program's by a relative error of at most 0.015.
Values may be sent and summed in bfloat16 or wider, within the bound.
A program may use at most 192 MiB of HBM per device.

```python
import math
import jax
import jax.numpy as jnp
import numpy as np
from jax import lax

D = 8192
HEAD = 128
QPK = 8
PROBLEMS = 8
BEAM_DEV = 16
STEP = 64
CTX = 512
QDIM = 8192
KVD = 1024
BEAMS = 256
CAP = 2
N_DP = 16
N_TENSOR = 8


def clipped(key, dims_shape, limit_value):
    return jnp.clip(jax.random.normal(key, dims_shape, jnp.float32), -limit_value, limit_value)


def shifted_pairs(key, dims_shape):
    noise_values = clipped(key, dims_shape, 6.0)
    return noise_values


def draw_queries(key, part):
    key = jax.random.fold_in(key, 11)
    base_key = jax.random.fold_in(key, 0)
    noise_values = clipped(base_key, (BEAMS, STEP, QDIM // HEAD, HEAD), 6.0)
    values = noise_values
    return values.reshape(BEAMS, STEP, QDIM).astype(jnp.bfloat16)


def draw_fresh_kv(key, part):
    key = jax.random.fold_in(key, 23)
    values = shifted_pairs(key, (BEAMS, 2, STEP, KVD))
    return values.astype(jnp.bfloat16)


def draw_kv_cache(key, part):
    key = jax.random.fold_in(key, 37)
    values = shifted_pairs(key, (BEAMS, 2, CTX, KVD))
    return values.astype(jnp.bfloat16)


def scaled_rows(key, row_low, row_high):
    row_key, column_key = jax.random.split(key)
    row_scale = jnp.exp(jax.random.uniform(row_key, (BEAMS, STEP, 1), jnp.float32, math.log(row_low), math.log(row_high)))
    rising = jnp.exp(math.log(3.0) * jnp.arange(D, dtype=jnp.float32) / D)
    column_scale = rising * jnp.exp(jax.random.uniform(column_key, (D,), jnp.float32, 0.0, math.log(3.5)))
    return row_scale * column_scale[None, None, :]


def draw_residual(key, part):
    key = jax.random.fold_in(key, 41)
    noise_key, scale_key = jax.random.split(key)
    noise_values = clipped(noise_key, (BEAMS, STEP, D), 4.0)
    values = noise_values * scaled_rows(scale_key, 0.3, 3.0)
    return values.astype(jnp.bfloat16)


def plant(drawn, rng, low, high):
    longest = drawn.shape.index(max(drawn.shape))
    spots = []
    for shift in (0, 1):
        where = [jax.random.randint(jax.random.fold_in(rng, axis), (), 0, length) for axis, length in enumerate(drawn.shape)]
        where[longest] = (where[longest] + shift) % drawn.shape[longest]
        spots.append(tuple(where))
    return drawn.at[spots[0]].set(low).at[spots[1]].set(high)


def level_of(rng, extent, pieces, smallest, high):
    loudness = 1.0
    for dim, blocks in pieces:
        heights = jax.random.uniform(jax.random.fold_in(jax.random.fold_in(rng, 6), dim), (blocks,), jnp.float32, smallest / len(pieces), high / len(pieces))
        loudness = loudness * jnp.repeat(jnp.exp(heights), extent[dim] // blocks).reshape((-1,) + (1,) * (len(extent) - 1 - dim))
    return loudness


def split_up(amount, total, most, skew):
    portions = [(1 << 20) // math.isqrt(rank ** skew) + 1 for rank in range(2, amount + 1)]
    spare, holding = total - most - (amount - 1), [1] * (amount - 1)
    while spare > 0:
        candidates = [i for i in range(amount - 1) if holding[i] < most]
        pool, left = sum([portions[i] for i in candidates]), spare
        for i in candidates:
            addition = min(most - holding[i], max(1, left * portions[i] // pool), spare)
            holding[i] = holding[i] + addition
            spare = spare - addition
    return np.array([most] + holding)


def ragged_sizes(own_key, number_of, total, most, skew):
    if number_of == 2:
        one = jax.random.randint(own_key, (), max(1, total - most), min(most, total - 1) + 1)
        return jnp.stack([one, total - one])
    sizes = jnp.asarray(split_up(number_of, total, most, skew), jnp.int32)
    pairs = (number_of - 1) // 2
    source_of, taker = sizes[1:1 + 2 * pairs:2], sizes[2:2 + 2 * pairs:2]
    slack = jnp.minimum(source_of - 1, most - taker)
    passed = jax.random.randint(jax.random.fold_in(own_key, 1), (pairs,), 0, 1 << 20) % (slack + 1)
    sizes = sizes.at[1:1 + 2 * pairs:2].set(source_of - passed).at[2:2 + 2 * pairs:2].set(taker + passed)
    return sizes[jax.random.permutation(jax.random.fold_in(own_key, 2), number_of)]


def shared_out(rng, own, number, rows, amount, top, bound, skew):
    ranking = jax.random.permutation(rng, amount)
    crowded, common = shares(amount, rows * top, bound, skew, True), shares(amount, rows * top, bound, skew, False)
    places = jnp.arange(amount)

    def named(sizes, offset_by):
        used = int((sizes > 0).sum())
        fixed = max(1, used // 4)
        moved = fixed + (places - fixed + offset_by * (used - fixed)) % max(1, amount - fixed)
        return jnp.zeros((amount,), jnp.int32).at[ranking[jnp.where(places < fixed, places, moved)]].set(jnp.asarray(sizes, jnp.int32))

    sizes = jnp.where(number % 4 == 0, named(crowded, number // 4), named(common, number - number // 4 - 1))
    mixed = jax.random.permutation(jax.random.fold_in(own, 3), amount)
    source_of, sink = mixed[0:amount // 2 * 2:2], mixed[1:amount // 2 * 2:2]
    margin = jnp.minimum(sizes[source_of] - 1, bound - sizes[sink]) // 2
    margin = jnp.where((source_of == ranking[0]) | (sink == ranking[0]) | (sizes[sink] == 0), 0, jnp.maximum(margin, 0))
    moved = jax.random.randint(jax.random.fold_in(own, 4), (amount // 2,), 0, 1 << 20) % (margin + 1)
    sizes = sizes.at[source_of].add(-moved).at[sink].add(moved)
    labels = jnp.searchsorted(jnp.cumsum(sizes), jnp.arange(rows * top), side="right").astype(jnp.int32)
    table = labels.reshape(top, rows).T
    table = table[jax.random.permutation(jax.random.fold_in(own, 1), rows)]
    offset_by = jax.random.randint(jax.random.fold_in(own, 2), (rows, 1), 0, top)
    return jnp.take_along_axis(table, (jnp.arange(top)[None, :] + offset_by) % top, axis=1)


def shares(count, total, limit, skew, full):
    portions = [(1 << 20) // math.isqrt(rank ** skew) + 1 for rank in range(1, count + 1)]
    largest = limit if full else min(limit, max(-(-total // count), total * portions[0] // sum(portions)))
    least = 1 if total - largest >= count - 1 else 0
    holding, spare = [largest] + [least] * (count - 1), total - largest - least * (count - 1)
    while spare > 0:
        movable = [i for i in range(1, count) if holding[i] < largest] or [i for i in range(1, count) if holding[i] < limit]
        whole, budget = sum([portions[i] for i in movable]), spare
        for i in movable:
            more = min(limit - holding[i], max(1, budget * portions[i] // whole), spare)
            holding[i] = holding[i] + more
            spare = spare - more
    return np.array(holding)


def scatter_about(key, extent, scale, bound, cuts=(), kind=jnp.bfloat16):
    gain = level_of(key, extent, cuts, -0.22, 0.18) if cuts else 1.0
    array = jax.random.normal(key, extent, jnp.float32) * scale * gain
    return jnp.minimum(jnp.maximum(array, -bound), bound).astype(kind)


def setup_inputs(seed: int = 0) -> dict:
    key_list = jax.random.split(jax.random.key(seed), 10)
    queries = draw_queries(jax.random.fold_in(key_list[9], 71), 0)
    fresh_kv = draw_fresh_kv(jax.random.fold_in(key_list[9], 71), 0)
    kv_cache = draw_kv_cache(jax.random.fold_in(key_list[9], 71), 0)
    parent_device_keys = jax.random.split(jax.random.fold_in(key_list[3], 1), BEAMS // BEAM_DEV)
    parent_device_turns = jax.random.permutation(jax.random.fold_in(key_list[3], 3), BEAMS // BEAM_DEV)
    parent_device = jax.vmap(lambda own, number: shared_out(jax.random.fold_in(key_list[3], 2), own, number, BEAM_DEV, N_DP, 1, CAP, 2))(parent_device_keys, parent_device_turns).reshape((BEAMS, 1))
    parent_rank = plant(jax.random.randint(key_list[4], (BEAMS,), 0, BEAM_DEV // PROBLEMS), jax.random.fold_in(key_list[4], 1), 0, (BEAM_DEV // PROBLEMS) - 1).astype(jnp.int32)
    cache_length = ragged_sizes(key_list[5], PROBLEMS, PROBLEMS * CTX * 5 // 8, CTX, 2).astype(jnp.int32)
    out_weight = scatter_about(key_list[6], (QDIM, D), (QDIM // 256) ** -0.5, 1.0, ((0, 8),))
    residual = draw_residual(jax.random.fold_in(key_list[9], 71), 0)
    norm_gain = jnp.clip(1.0 + 0.15 * jax.random.normal(key_list[8], (D,), jnp.float32), 0.25, 1.75).astype(jnp.bfloat16)
    return {"queries": queries, "fresh_kv": fresh_kv, "kv_cache": kv_cache, "parent_device": parent_device, "parent_rank": parent_rank, "cache_length": cache_length, "out_weight": out_weight, "residual": residual, "norm_gain": norm_gain}


def attend(queries, fresh_kv, kv_cache, lengths):
    beam_count = queries.shape[0]
    step_count = queries.shape[1]
    cache_positions = kv_cache.shape[2]
    kv_heads = fresh_kv.shape[3] // HEAD
    scaling = 1.0 / math.sqrt(HEAD)
    grouped = queries.astype(jnp.float32).reshape(beam_count, step_count, kv_heads, QPK, HEAD)
    cached_keys = kv_cache[:, 0].astype(jnp.float32).reshape(beam_count, cache_positions, kv_heads, HEAD)
    cached_values = kv_cache[:, 1].astype(jnp.float32).reshape(beam_count, cache_positions, kv_heads, HEAD)
    fresh_keys = fresh_kv[:, 0].astype(jnp.float32).reshape(beam_count, step_count, kv_heads, HEAD)
    fresh_values = fresh_kv[:, 1].astype(jnp.float32).reshape(beam_count, step_count, kv_heads, HEAD)
    cache_scores = jnp.einsum('bsngd,btnd->bngst', grouped, cached_keys) * scaling
    fresh_scores = jnp.einsum('bsngd,bund->bngsu', grouped, fresh_keys) * scaling
    live_mask = (jnp.arange(cache_positions, dtype=jnp.int32)[None, :] < lengths[:, None]).reshape(beam_count, 1, 1, 1, cache_positions)
    causal_mask = jnp.arange(step_count, dtype=jnp.int32)[:, None] >= jnp.arange(step_count, dtype=jnp.int32)[None, :]
    cache_scores = jnp.where(live_mask, cache_scores, -jnp.inf)
    fresh_scores = jnp.where(causal_mask, fresh_scores, -jnp.inf)
    highest = jnp.maximum(lax.optimization_barrier(jnp.max(cache_scores, axis=-1)), lax.optimization_barrier(jnp.max(fresh_scores, axis=-1)))[..., None]
    cache_probs = jnp.exp(cache_scores - highest)
    fresh_probs = jnp.exp(fresh_scores - highest)
    denominator = lax.optimization_barrier(jnp.sum(cache_probs, axis=-1, keepdims=True)) + lax.optimization_barrier(jnp.sum(fresh_probs, axis=-1, keepdims=True))
    cache_weights = lax.optimization_barrier((cache_probs / denominator).astype(jnp.bfloat16)).astype(jnp.float32)
    fresh_weights = lax.optimization_barrier((fresh_probs / denominator).astype(jnp.bfloat16)).astype(jnp.float32)
    combined = jnp.einsum('bngst,btnd->bsngd', cache_weights, cached_values) + jnp.einsum('bngsu,bund->bsngd', fresh_weights, fresh_values)
    return combined.astype(jnp.bfloat16).reshape(beam_count, step_count, kv_heads * QPK * HEAD)

def reference(queries, fresh_kv, kv_cache, parent_device, parent_rank, cache_length, out_weight, residual, norm_gain):
    beam_index = jnp.arange(BEAMS, dtype=jnp.int32)
    parent = (parent_device[:, 0] * BEAM_DEV + parent_rank * PROBLEMS + beam_index % PROBLEMS).astype(jnp.int32)
    length = cache_length[beam_index % PROBLEMS]

    def one_beam(beam_items):
        beam_query, beam_fresh, source, live_count = beam_items
        beam_cache = lax.dynamic_index_in_dim(kv_cache, source, 0, keepdims=True)
        return attend(beam_query[None], beam_fresh[None], beam_cache, live_count[None])[0]
    mixed_heads = lax.map(one_beam, (queries, fresh_kv, parent, length))
    flat_rows = mixed_heads.reshape(BEAMS * STEP, QDIM)
    block_width = QDIM // N_TENSOR
    projected = jnp.zeros((BEAMS * STEP, D), jnp.float32)
    for part_index in range(N_TENSOR):
        partial_value = jnp.dot(flat_rows[:, part_index * block_width:(part_index + 1) * block_width], out_weight[part_index * block_width:(part_index + 1) * block_width], preferred_element_type=jnp.float32).astype(jnp.bfloat16)
        partial_value = lax.optimization_barrier(partial_value)
        projected = projected + partial_value.astype(jnp.float32)
    attended = residual.reshape(BEAMS * STEP, D).astype(jnp.float32) + projected
    squares = lax.optimization_barrier(jnp.mean(attended * attended, axis=1, keepdims=True))
    normed = attended * lax.rsqrt(squares + 1e-06) * norm_gain.astype(jnp.float32)[None, :]
    return normed.astype(jnp.bfloat16).reshape(BEAMS, STEP, D)
```

```python
import functools
import math

import jax
import jax.numpy as jnp
from jax import lax
from jax.experimental import pallas as pl
from jax.experimental.pallas import tpu as pltpu
from jax.sharding import PartitionSpec as P

MESH = pl.DeviceIdType.MESH
HEAD = 128
BLK = 16
LANES = 128
EPS = 1e-06
F32 = jnp.float32
BF16 = jnp.bfloat16
STRIDE = 7


class Plan:
    def __init__(self, n, tensor, beams, step, ctx, width, problems, model):
        self.n, self.tensor, self.zs = n, tensor, tensor // 2
        self.beams, self.step, self.ctx, self.width = beams, step, ctx, width
        self.problems, self.ranks, self.model = problems, beams // problems, model
        self.side = math.isqrt(n)
        total = problems * ctx * 5 // 8
        rest = total - ctx
        before = [
            (rest * j // (problems - 1) + (BLK - 1) * j) // BLK for j in range(problems)
        ]
        before.append(ctx // BLK + before[problems - 1])
        ends = [1, 3, 5, 7, 8] if problems == 8 else list(range(1, problems + 1))
        self.chunks, self.turns = [], []
        low, turn = 0, 0
        for end in ends:
            last = -(-before[end] // n)
            self.chunks.append((low, end))
            self.turns.append((turn, last))
            low, turn = end, last
        self.slots = turn * n
        self.blocks = ctx // BLK
        self.most = []
        for j in range(problems):
            bound = rest // (problems - 1 - j) if j < problems - 1 else ctx
            self.most.append(min(ctx, -(-bound // LANES) * LANES))
        self.rows = max(
            [self.slots * BLK] + [before[j] * BLK + self.most[j] for j in range(problems)]
        )
        self.rows = -(-self.rows // BLK) * BLK
        self.row_most = max(e - s for s, e in self.chunks) * self.ranks * step
        self.turn_most = max(e - s for s, e in self.turns)


def kernel(plan, names, *refs):
    r = dict(zip(names, refs))
    n, zs, tensor = plan.n, plan.zs, plan.tensor
    ranks, problems, step, width = plan.ranks, plan.problems, plan.step, plan.width
    heads = width // HEAD
    side = plan.side
    count = len(plan.chunks)
    slots = plan.slots
    me = lax.axis_index("dp")
    mine = lax.axis_index("tensor")
    my_y, my_x = me // side, me % side
    my_z, my_core = mine // 2, mine % 2
    tab, reqs = r["tab"], r["reqs"]
    at_order, at_off, at_len, at_rank = (2 * slots + problems * i for i in range(4))

    def plane_peer(index):
        hop = (index * STRIDE) % n
        there = ((my_y + hop // side) % side) * side + (my_x + hop % side) % side
        return hop, there

    def tensor_peer(hop):
        return (mine + hop) % tensor

    def chip_at(hop):
        return (my_z + hop) % zs

    loads = {}
    for i, name in enumerate(("kv", "q", "fresh", "wt", "res")):
        loads[name] = pltpu.make_async_copy(r[name + "_h"], r[name], r["load_sem"].at[i])
        loads[name].start()

    barrier = pltpu.get_barrier_semaphore()

    @pl.loop(1, n)
    def _(index):
        hop, there = plane_peer(index)
        pl.semaphore_signal(barrier, inc=1, device_id=(there, mine), device_id_type=MESH)

    @pl.loop(1, tensor)
    def _(hop):
        pl.semaphore_signal(
            barrier, inc=1, device_id=(me, tensor_peer(hop)), device_id_type=MESH
        )

    loads["kv"].wait()
    pl.semaphore_wait(barrier, n - 1 + tensor - 1)

    def request_copy(index):
        hop, there = plane_peer(index)
        return pltpu.make_async_remote_copy(
            src_ref=r["req"],
            dst_ref=r["reqv"].at[me],
            send_sem=r["rq_s"].at[hop],
            recv_sem=r["rq_r"].at[hop],
            device_id=(there, mine),
            device_id_type=MESH,
        )

    @pl.loop(1, n)
    def _(index):
        request_copy(index).start()

    r["reqv"][me] = r["req"][...]

    def spread_copy(c, index):
        hop, there = plane_peer(index)
        lo, hi = plan.turns[c]
        return pltpu.make_async_remote_copy(
            src_ref=r["send1"].at[c % 2, there, pl.ds(0, ranks), pl.ds(0, hi - lo)],
            dst_ref=r[f"stash{c}"].at[pl.ds(me * ranks, ranks)],
            send_sem=r["p1_s"].at[c, hop],
            recv_sem=r["p1_r"].at[c, hop],
            device_id=(there, mine),
            device_id_type=MESH,
        )

    def fetch_copy(c, index):
        hop, there = plane_peer(index)
        lo, hi = plan.turns[c]
        return pltpu.make_async_remote_copy(
            src_ref=r["send2"].at[c % 2, there, pl.ds(0, ranks), pl.ds(0, hi - lo)],
            dst_ref=r[f"got{c}"].at[me],
            send_sem=r["p2_s"].at[c, hop],
            recv_sem=r["p2_r"].at[c, hop],
            device_id=(there, mine),
            device_id_type=MESH,
        )

    def each_peer(make, c, what):
        @pl.loop(1, n)
        def _(index):
            getattr(make(c, index), what)()

    def spread(c):
        lo, hi = plan.turns[c]
        if c >= 2:
            each_peer(spread_copy, c - 2, "wait_send")

        @pl.loop(0, n)
        def _(k):
            for i in range(lo, hi):
                problem = tab[i * n + k]
                block = tab[slots + i * n + k]
                for rank in range(ranks):
                    r["send1"][c % 2, k, rank, i - lo] = r["kv"][
                        rank * problems + problem, :, block
                    ]

        each_peer(spread_copy, c, "start")
        for rank in range(ranks):
            r[f"stash{c}"][me * ranks + rank] = r["send1"][c % 2, me, rank, : hi - lo]

    def fetch(c):
        lo, hi = plan.turns[c]
        each_peer(spread_copy, c, "wait_recv")
        if c >= 2:
            each_peer(fetch_copy, c - 2, "wait_send")

        @pl.loop(0, n)
        def _(child):
            for i in range(lo, hi):
                problem = tab[i * n + me]
                for slot in range(ranks):
                    parent = reqs[child, 0, slot * problems + problem]
                    r["send2"][c % 2, child, slot, i - lo] = r[f"stash{c}"][parent, i - lo]

        each_peer(fetch_copy, c, "start")
        r[f"got{c}"][me] = r["send2"][c % 2, me, :, : hi - lo]

    def unpack(c):
        lo, hi = plan.turns[c]
        each_peer(fetch_copy, c, "wait_recv")

        @pl.loop(0, n)
        def _(k):
            for i in range(lo, hi):
                for slot in range(ranks):
                    for part, name in enumerate(("kbuf", "vbuf")):
                        r[name][slot, i * n + k] = r[f"got{c}"][k, slot, i - lo, part]

    group = min(4, heads)
    factor = math.log2(math.e) / math.sqrt(HEAD)
    nt = (((1,), (1,)), ((), ()))

    def attend(c):
        first, last = plan.chunks[c]
        span = plan.most[last - 1]

        @pl.loop(0, (last - first) * ranks)
        def _(e):
            j = first + e // ranks
            slot = e % ranks
            beam = slot * problems + tab[at_order + j]
            start = tab[at_off + j]
            live = tab[at_len + j]
            keys, values = (
                jnp.concatenate([r[name][slot, start + i] for i in range(span // BLK)], axis=0)
                for name in ("kbuf", "vbuf")
            )
            new_keys, new_values = r["fresh"][beam, 0], r["fresh"][beam, 1]
            values = jnp.concatenate([values, jnp.ones_like(values)], axis=1)
            new_values = jnp.concatenate([new_values, jnp.ones_like(new_values)], axis=1)
            query = r["q"][beam]
            place = pl.multiple_of(e * step, step)
            for g in range(0, heads, group):
                part = jnp.concatenate(
                    [query[:, (g + h) * HEAD : (g + h + 1) * HEAD] for h in range(group)], axis=0
                )
                old = lax.dot_general(part, keys, nt, preferred_element_type=F32)
                new = lax.dot_general(part, new_keys, nt, preferred_element_type=F32)
                where = lax.broadcasted_iota(jnp.int32, old.shape, 1)
                old = jnp.where(where < live, old, -1e30)
                token = lax.broadcasted_iota(jnp.int32, new.shape, 0) % step
                other = lax.broadcasted_iota(jnp.int32, new.shape, 1)
                new = jnp.where(other <= token, new, -1e30)
                top = jnp.maximum(
                    jnp.max(old, axis=1, keepdims=True), jnp.max(new, axis=1, keepdims=True)
                )
                old = jnp.exp2((old - top) * factor).astype(BF16)
                new = jnp.exp2((new - top) * factor).astype(BF16)
                out = jnp.dot(old, values, preferred_element_type=F32)
                out = out + jnp.dot(new, new_values, preferred_element_type=F32)
                out = (out[:, :HEAD] / out[:, HEAD:]).astype(BF16)
                for h in range(group):
                    r["mixed"][pl.ds(place, step), (g + h) * HEAD : (g + h + 1) * HEAD] = out[
                        h * step : (h + 1) * step
                    ]

    def rows_of(c):
        first, last = plan.chunks[c]
        return (last - first) * ranks * step

    tile = min(256, width)

    def project(c, block, target):
        rows = rows_of(c)

        @pl.loop(0, width // tile)
        def _(k):
            here = pl.multiple_of(k * tile, tile)
            column = pl.multiple_of(block * width + here, tile)
            value = jnp.dot(
                r["mixed"][:rows, :], r["wt"][:, pl.ds(column, tile)], preferred_element_type=F32
            )
            target[:rows, pl.ds(here, tile)] = value.astype(BF16)

    pending = {}

    def core_copy(c, hop):
        rows = rows_of(c)
        return pltpu.make_async_remote_copy(
            src_ref=r["csend"].at[hop, pl.ds(0, rows)],
            dst_ref=r["crecv"].at[c % 2, hop, pl.ds(0, rows)],
            send_sem=r["c_s"].at[hop],
            recv_sem=r["c_r"].at[c, hop],
            device_id=(me, my_z * 2 + 1 - my_core),
            device_id_type=MESH,
        )

    def block_for(c, hop):
        if c >= 1:
            pending["core", c - 1, hop].wait_send()
        project(c, chip_at(hop) * 2 + 1 - my_core, r["csend"].at[hop])
        pending["core", c, hop] = core_copy(c, hop)
        pending["core", c, hop].start()
        project(c, chip_at(hop) * 2 + my_core, r["own"].at[c % 2, hop])

    def z_copy(c, kind, way):
        rows = rows_of(c)
        hop = (1, zs - 1)[way]
        if kind == "t":
            src = r["tsend"].at[pl.ds(way * (rows // 2), rows // 2)]
            dst = r[f"trecv{c}"].at[way]
        else:
            src = r["dsend"].at[way, pl.ds(0, rows)]
            dst = r[f"drecv{c}"].at[way]
        return pltpu.make_async_remote_copy(
            src_ref=src,
            dst_ref=dst,
            send_sem=r[kind + "_s"].at[way],
            recv_sem=r[kind + "_r"].at[c, way],
            device_id=(me, chip_at(hop) * 2 + my_core),
            device_id_type=MESH,
        )

    opposite = zs // 2
    piece = 32

    def send_far(c):
        rows = rows_of(c)
        pending["core", c, opposite].wait_recv()
        if c >= 1:
            for way in range(2):
                pending["t", c - 1, way].wait_send()

        @pl.loop(0, rows // piece)
        def _(i):
            at = pl.ds(pl.multiple_of(i * piece, piece), piece)
            value = r["own"][c % 2, opposite, at, :].astype(F32)
            value = value + r["crecv"][c % 2, opposite, at, :].astype(F32)
            r["tsend"][at, :] = value.astype(BF16)

        for way in range(2):
            pending["t", c, way] = z_copy(c, "t", way)
            pending["t", c, way].start()

    def send_near(c):
        rows = rows_of(c)
        half = rows // 2
        for way in range(2):
            hop = (1, zs - 1)[way]
            pending["core", c, hop].wait_recv()
            pending["t", c, way].wait_recv()
            if c >= 1:
                pending["d", c - 1, way].wait_send()

            @pl.loop(0, half // piece)
            def _(i):
                at = pl.ds(pl.multiple_of((1 - way) * half + i * piece, piece), piece)
                value = r["own"][c % 2, hop, at, :].astype(F32)
                value = value + r["crecv"][c % 2, hop, at, :].astype(F32)
                r["dsend"][way, at, :] = value.astype(BF16)

            @pl.loop(0, half // piece)
            def _(i):
                start = pl.multiple_of(i * piece, piece)
                at = pl.ds(pl.multiple_of(way * half + i * piece, piece), piece)
                value = r["own"][c % 2, hop, at, :].astype(F32)
                value = value + r["crecv"][c % 2, hop, at, :].astype(F32)
                value = value + r[f"trecv{c}"][way, pl.ds(start, piece), :].astype(F32)
                r["dsend"][way, at, :] = value.astype(BF16)

            pending["d", c, way] = z_copy(c, "d", way)
            pending["d", c, way].start()

    def square_copy(c, hop):
        return pltpu.make_async_remote_copy(
            src_ref=r[f"sq{c}"],
            dst_ref=r[f"sqr{c}"].at[mine],
            send_sem=r["s_s"].at[c, hop],
            recv_sem=r["s_r"].at[c, hop],
            device_id=(me, tensor_peer(hop)),
            device_id_type=MESH,
        )

    def finish(c):
        first, last = plan.chunks[c]
        pending["core", c, 0].wait_recv()
        for way in range(2):
            pending["d", c, way].wait_recv()

        @pl.loop(0, (last - first) * ranks)
        def _(e):
            j = first + e // ranks
            slot = e % ranks
            beam = slot * problems + tab[at_order + j]
            for low in range(0, step, 32):
                at = pl.ds(pl.multiple_of(e * step + low, 32), 32)
                value = r["own"][c % 2, 0, at, :].astype(F32)
                value = value + r["crecv"][c % 2, 0, at, :].astype(F32)
                value = value + r[f"drecv{c}"][0, at, :].astype(F32)
                value = value + r[f"drecv{c}"][1, at, :].astype(F32)
                value = value + r["res"][beam, low : low + 32, :].astype(F32)
                place = pl.ds(pl.multiple_of(slot * step + low, 32), 32)
                r["att"][j, place, :] = value
                value = value * value
                total = value[:, :LANES]
                for k in range(LANES, width, LANES):
                    total = total + value[:, k : k + LANES]
                r["sums"][e // ranks, place, :] = total

        for k in range(last - first):
            line = jnp.sum(r["sums"][k].T, axis=0, keepdims=True)
            r[f"sq{c}"][k] = jnp.broadcast_to(line, (8, line.shape[1]))
        r[f"sqr{c}"][mine] = r[f"sq{c}"][...]

        @pl.loop(1, tensor)
        def _(hop):
            square_copy(c, hop).start()

        if c + 2 < count:
            pl.semaphore_signal(
                r["credit"],
                inc=1,
                device_id=(me, my_z * 2 + 1 - my_core),
                device_id_type=MESH,
            )

    def project_all(c):
        if c >= 2:
            finish(c - 2)
            pl.semaphore_wait(r["credit"], 1)
        hops = [opposite, 1, zs - 1, 0]
        block_for(c, hops[0])
        block_for(c, hops[1])
        send_far(c)
        block_for(c, hops[2])
        block_for(c, hops[3])

    spread(0)
    if count > 1:
        spread(1)

    @pl.loop(1, n)
    def _(index):
        request_copy(index).wait_recv()

    table = pltpu.make_async_copy(r["reqv"], reqs, r["table_sem"])
    table.start()

    @pl.loop(0, plan.rows // BLK)
    def _(i):
        for name in ("kbuf", "vbuf"):
            for slot in range(ranks):
                r[name][slot, i] = jnp.zeros((BLK, HEAD), BF16)

    table.wait()
    fetch(0)
    if count > 2:
        spread(2)
    for name in ("q", "fresh", "wt", "res"):
        loads[name].wait()

    for c in range(count):
        if c + 1 < count:
            fetch(c + 1)
        if c + 3 < count:
            spread(c + 3)
        unpack(c)
        attend(c)
        if c >= 1:
            send_near(c - 1)
        project_all(c)
    send_near(count - 1)
    if count > 1:
        finish(count - 2)
    finish(count - 1)

    for c, (first, last) in enumerate(plan.chunks):

        @pl.loop(1, tensor)
        def _(hop):
            square_copy(c, hop).wait_recv()

        for k in range(last - first):
            line = r[f"sqr{c}"][0, k]
            for t in range(1, tensor):
                line = line + r[f"sqr{c}"][t, k]
            line = lax.rsqrt(line / plan.model + EPS)
            wide = jnp.broadcast_to(line[0:1, :], (LANES, line.shape[1]))
            r["scale"][first + k] = wide.T

    def out_copy(problem, slot):
        beam = slot * problems + problem
        return pltpu.make_async_copy(
            r["res"].at[beam], r["out_h"].at[beam], r["out_sem"].at[beam]
        )

    @pl.loop(0, problems)
    def _(problem):
        j = tab[at_rank + problem]
        for slot in range(ranks):
            for low in range(0, step, 32):
                at = slice(slot * step + low, slot * step + low + 32)
                scale = r["scale"][j, at, :]
                for k in range(0, width, LANES):
                    value = r["att"][j, at, k : k + LANES] * scale
                    value = value * r["gain"][:, k : k + LANES].astype(F32)
                    r["res"][slot * problems + problem, low : low + 32, k : k + LANES] = (
                        value.astype(BF16)
                    )
            out_copy(problem, slot).start()

    @pl.loop(0, problems)
    def _(problem):
        for slot in range(ranks):
            out_copy(problem, slot).wait()

    @pl.loop(1, n)
    def _(index):
        request_copy(index).wait_send()

    for c in range(max(0, count - 2), count):
        each_peer(spread_copy, c, "wait_send")
        each_peer(fetch_copy, c, "wait_send")
    for hop in range(zs):
        pending["core", count - 1, hop].wait_send()
    for way in range(2):
        pending["t", count - 1, way].wait_send()
        pending["d", count - 1, way].wait_send()
    for c in range(count):

        @pl.loop(1, tensor)
        def _(hop):
            square_copy(c, hop).wait_send()


def tables(plan, cache_length, parent_device, parent_rank):
    problems = plan.problems
    lengths = cache_length.astype(jnp.int32)
    ids = jnp.arange(problems, dtype=jnp.int32)
    below = (lengths[None, :] < lengths[:, None]) | (
        (lengths[None, :] == lengths[:, None]) & (ids[None, :] < ids[:, None])
    )
    rank = jnp.sum(below.astype(jnp.int32), axis=1)
    chosen = (rank[None, :] == ids[:, None]).astype(jnp.int32)
    order = jnp.sum(chosen * ids[None, :], axis=1)
    live = jnp.sum(chosen * lengths[None, :], axis=1)
    used = (lengths + BLK - 1) // BLK
    start = jnp.sum(jnp.where(rank[None, :] < ids[:, None], used[None, :], 0), axis=1)
    slot = jnp.arange(plan.slots, dtype=jnp.int32)
    turn = jnp.sum((start[None, 1:] <= slot[:, None]).astype(jnp.int32), axis=1)
    mine = (turn[:, None] == ids[None, :]).astype(jnp.int32)
    problem = jnp.sum(mine * order[None, :], axis=1)
    block = jnp.clip(slot - jnp.sum(mine * start[None, :], axis=1), 0, plan.blocks - 1)
    tab = jnp.concatenate([problem, block, order, start, live, rank])
    wanted = parent_device[:, 0] * plan.ranks + parent_rank
    req = jnp.zeros((8, LANES), jnp.int32).at[0, : plan.beams].set(wanted)
    return tab, req


def on_device(
    queries, fresh_kv, kv_cache, parent_device, parent_rank, cache_length, out_weight, residual,
    norm_gain,
):
    n, tensor = lax.axis_size("dp"), lax.axis_size("tensor")
    beams, step, width = queries.shape
    ctx = kv_cache.shape[2]
    plan = Plan(n, tensor, beams, step, ctx, width, cache_length.shape[0], width * tensor)
    tab, req = tables(plan, cache_length, parent_device, parent_rank)
    count, ranks, most = len(plan.chunks), plan.ranks, plan.row_most
    blocks = kv_cache.reshape(beams, 2, plan.blocks, BLK, HEAD)

    smem = pl.BlockSpec(memory_space=pltpu.SMEM)
    vmem = pl.BlockSpec(memory_space=pltpu.VMEM)
    hbm = pl.BlockSpec(memory_space=pl.ANY)
    inputs = [
        ("tab", tab, smem),
        ("req", req, vmem),
        ("gain", norm_gain.reshape(1, width), vmem),
        ("q_h", queries, hbm),
        ("fresh_h", fresh_kv, hbm),
        ("kv_h", blocks, hbm),
        ("wt_h", out_weight, hbm),
        ("res_h", residual, hbm),
    ]
    dma = lambda *shape: pltpu.SemaphoreType.DMA(shape)
    scratch = [
        ("q", pltpu.VMEM(queries.shape, BF16)),
        ("fresh", pltpu.VMEM(fresh_kv.shape, BF16)),
        ("kv", pltpu.VMEM(blocks.shape, BF16)),
        ("wt", pltpu.VMEM(out_weight.shape, BF16)),
        ("res", pltpu.VMEM(residual.shape, BF16)),
        ("kbuf", pltpu.VMEM((ranks, plan.rows // BLK, BLK, HEAD), BF16)),
        ("vbuf", pltpu.VMEM((ranks, plan.rows // BLK, BLK, HEAD), BF16)),
        ("send1", pltpu.VMEM((2, n, ranks, plan.turn_most, 2, BLK, HEAD), BF16)),
        ("send2", pltpu.VMEM((2, n, ranks, plan.turn_most, 2, BLK, HEAD), BF16)),
        ("reqv", pltpu.VMEM((n, 8, LANES), jnp.int32)),
        ("reqs", pltpu.SMEM((n, 8, LANES), jnp.int32)),
        ("mixed", pltpu.VMEM((most, width), BF16)),
        ("own", pltpu.VMEM((2, plan.zs, most, width), BF16)),
        ("csend", pltpu.VMEM((plan.zs, most, width), BF16)),
        ("crecv", pltpu.VMEM((2, plan.zs, most, width), BF16)),
        ("tsend", pltpu.VMEM((most, width), BF16)),
        ("dsend", pltpu.VMEM((2, most, width), BF16)),
        ("att", pltpu.VMEM((plan.problems, ranks * step, width), F32)),
        ("sums", pltpu.VMEM((most // (ranks * step), ranks * step, LANES), F32)),
        ("scale", pltpu.VMEM((plan.problems, ranks * step, LANES), F32)),
        ("load_sem", dma(5)),
        ("table_sem", pltpu.SemaphoreType.DMA),
        ("rq_s", dma(n)),
        ("rq_r", dma(n)),
        ("p1_s", dma(count, n)),
        ("p1_r", dma(count, n)),
        ("p2_s", dma(count, n)),
        ("p2_r", dma(count, n)),
        ("c_s", dma(plan.zs)),
        ("c_r", dma(count, plan.zs)),
        ("t_s", dma(2)),
        ("t_r", dma(count, 2)),
        ("d_s", dma(2)),
        ("d_r", dma(count, 2)),
        ("s_s", dma(count, tensor)),
        ("s_r", dma(count, tensor)),
        ("out_sem", dma(beams)),
        ("credit", pltpu.SemaphoreType.REGULAR),
    ]
    for c in range(count):
        (first, last), (lo, hi) = plan.chunks[c], plan.turns[c]
        rows = (last - first) * ranks * step
        scratch += [
            (f"stash{c}", pltpu.VMEM((n * ranks, hi - lo, 2, BLK, HEAD), BF16)),
            (f"got{c}", pltpu.VMEM((n, ranks, hi - lo, 2, BLK, HEAD), BF16)),
            (f"trecv{c}", pltpu.VMEM((2, rows // 2, width), BF16)),
            (f"drecv{c}", pltpu.VMEM((2, rows, width), BF16)),
            (f"sq{c}", pltpu.VMEM((last - first, 8, ranks * step), F32)),
            (f"sqr{c}", pltpu.VMEM((tensor, last - first, 8, ranks * step), F32)),
        ]
    names = [i[0] for i in inputs] + ["out_h"] + [s[0] for s in scratch]
    rows = beams * step
    return pl.pallas_call(
        functools.partial(kernel, plan, names),
        out_shape=jax.ShapeDtypeStruct(residual.shape, BF16),
        in_specs=[i[2] for i in inputs],
        out_specs=hbm,
        scratch_shapes=[s[1] for s in scratch],
        compiler_params=pltpu.CompilerParams(
            collective_id=0, has_side_effects=True, vmem_limit_bytes=64 * 1024 * 1024 - 4096
        ),
        cost_estimate=pl.CostEstimate(
            flops=2 * rows * width * width * tensor + 4 * rows * width * (ctx + step),
            bytes_accessed=30 * 1024 * 1024,
            transcendentals=rows * (width // HEAD) * (ctx + step),
        ),
        name="step_scoring",
    )(*[i[1] for i in inputs])


def solution(mesh):
    placed = (
        P("dp", None, "tensor"),
        P("dp", None, None, "tensor"),
        P("dp", None, None, "tensor"),
        P("dp", None),
        P("dp"),
        P(),
        P("tensor", None),
        P("dp", None, "tensor"),
        P("tensor"),
    )
    return jax.shard_map(
        on_device, mesh=mesh, in_specs=placed, out_specs=P("dp", None, "tensor"), check_vma=False
    )
```

```python
import functools
import math

import jax
import jax.numpy as jnp
from jax import lax
from jax.experimental import pallas as pl
from jax.experimental.pallas import tpu as pltpu
from jax.sharding import PartitionSpec as P

MESH = pl.DeviceIdType.MESH
HEAD = 128
BLK = 16
LANES = 128
EPS = 1e-06
F32 = jnp.float32
BF16 = jnp.bfloat16
STRIDE = 7


class Plan:
    def __init__(self, n, tensor, beams, step, ctx, width, problems, model):
        self.n, self.tensor, self.zs = n, tensor, tensor // 2
        self.beams, self.step, self.ctx, self.width = beams, step, ctx, width
        self.problems, self.ranks, self.model = problems, beams // problems, model
        self.side = math.isqrt(n)
        total = problems * ctx * 5 // 8
        rest = total - ctx
        before = [
            (rest * j // (problems - 1) + (BLK - 1) * j) // BLK for j in range(problems)
        ]
        before.append(ctx // BLK + before[problems - 1])
        ends = [1, 3, 5, 7, 8] if problems == 8 else list(range(1, problems + 1))
        self.chunks, self.turns = [], []
        low, turn = 0, 0
        for end in ends:
            last = -(-before[end] // n)
            self.chunks.append((low, end))
            self.turns.append((turn, last))
            low, turn = end, last
        self.slots = turn * n
        self.blocks = ctx // BLK
        self.most = []
        for j in range(problems):
            bound = rest // (problems - 1 - j) if j < problems - 1 else ctx
            self.most.append(min(ctx, -(-bound // LANES) * LANES))
        self.rows = max(
            [self.slots * BLK] + [before[j] * BLK + self.most[j] for j in range(problems)]
        )
        self.rows = -(-self.rows // BLK) * BLK
        self.row_most = max(e - s for s, e in self.chunks) * self.ranks * step
        self.turn_most = max(e - s for s, e in self.turns)


def kernel(plan, names, *refs):
    r = dict(zip(names, refs))
    n, zs, tensor = plan.n, plan.zs, plan.tensor
    ranks, problems, step, width = plan.ranks, plan.problems, plan.step, plan.width
    heads = width // HEAD
    side = plan.side
    count = len(plan.chunks)
    slots = plan.slots
    me = lax.axis_index("dp")
    mine = lax.axis_index("tensor")
    my_y, my_x = me // side, me % side
    my_z, my_core = mine // 2, mine % 2
    tab, reqs = r["tab"], r["reqs"]
    at_order, at_off, at_len, at_rank = (2 * slots + problems * i for i in range(4))

    def plane_peer(index):
        hop = (index * STRIDE) % n
        there = ((my_y + hop // side) % side) * side + (my_x + hop % side) % side
        return hop, there

    def tensor_peer(hop):
        return (mine + hop) % tensor

    def chip_at(hop):
        return (my_z + hop) % zs

    barrier = pltpu.get_barrier_semaphore()

    @pl.loop(1, n)
    def _(index):
        hop, there = plane_peer(index)
        pl.semaphore_signal(barrier, inc=1, device_id=(there, mine), device_id_type=MESH)

    @pl.loop(1, tensor)
    def _(hop):
        pl.semaphore_signal(
            barrier, inc=1, device_id=(me, tensor_peer(hop)), device_id_type=MESH
        )

    loads = {}
    for i, name in enumerate(("kv", "q", "fresh", "wt", "res")):
        loads[name] = pltpu.make_async_copy(r[name + "_h"], r[name], r["load_sem"].at[i])
    loads["kv"].start()

    lengths = [r["length"][p] for p in range(problems)]
    rank_of = []
    for p in range(problems):
        found = jnp.int32(0)
        for o in range(problems):
            if o != p:
                ahead = lengths[o] <= lengths[p] if o < p else lengths[o] < lengths[p]
                found = found + jnp.where(ahead, 1, 0)
        rank_of.append(found)
        tab[at_rank + p] = found
    starts = []
    for j in range(problems):
        which, long, start = jnp.int32(0), jnp.int32(0), jnp.int32(0)
        for p in range(problems):
            hit = rank_of[p] == j
            which = which + jnp.where(hit, p, 0)
            long = long + jnp.where(hit, lengths[p], 0)
            used = lax.div(lengths[p] + (BLK - 1), jnp.int32(BLK))
            start = start + jnp.where(rank_of[p] < j, used, 0)
        tab[at_order + j], tab[at_len + j], tab[at_off + j] = which, long, start
        starts.append(start)

    def place(lo, hi):
        @pl.loop(lo * n, hi * n)
        def _(slot):
            turn = jnp.int32(0)
            for j in range(1, problems):
                turn = turn + jnp.where(starts[j] <= slot, 1, 0)
            tab[slot] = tab[at_order + turn]
            block = slot - tab[at_off + turn]
            tab[slots + slot] = jnp.minimum(jnp.maximum(block, 0), plan.blocks - 1)

    lane = lax.broadcasted_iota(jnp.int32, (8, LANES), 1)
    wanted = jnp.zeros((8, LANES), jnp.int32)
    for b in range(plan.beams):
        value = r["device"][b] * ranks + r["rank"][b]
        wanted = jnp.where(lane == b, value, wanted)
    r["req"][...] = wanted

    pl.semaphore_wait(barrier, n - 1 + tensor - 1)

    def request_copy(index):
        hop, there = plane_peer(index)
        return pltpu.make_async_remote_copy(
            src_ref=r["req"],
            dst_ref=r["reqv"].at[me],
            send_sem=r["rq_s"].at[hop],
            recv_sem=r["rq_r"].at[hop],
            device_id=(there, mine),
            device_id_type=MESH,
        )

    @pl.loop(1, n)
    def _(index):
        request_copy(index).start()

    r["reqv"][me] = r["req"][...]

    def spread_copy(c, index):
        hop, there = plane_peer(index)
        lo, hi = plan.turns[c]
        return pltpu.make_async_remote_copy(
            src_ref=r["send1"].at[c % 2, there, pl.ds(0, ranks), pl.ds(0, hi - lo)],
            dst_ref=r[f"stash{c}"].at[pl.ds(me * ranks, ranks)],
            send_sem=r["p1_s"].at[c, hop],
            recv_sem=r["p1_r"].at[c, hop],
            device_id=(there, mine),
            device_id_type=MESH,
        )

    def fetch_copy(c, index):
        hop, there = plane_peer(index)
        lo, hi = plan.turns[c]
        return pltpu.make_async_remote_copy(
            src_ref=r["send2"].at[c % 2, there, pl.ds(0, ranks), pl.ds(0, hi - lo)],
            dst_ref=r[f"got{c}"].at[me],
            send_sem=r["p2_s"].at[c, hop],
            recv_sem=r["p2_r"].at[c, hop],
            device_id=(there, mine),
            device_id_type=MESH,
        )

    def each_peer(make, c, what):
        @pl.loop(1, n)
        def _(index):
            getattr(make(c, index), what)()

    def spread(c):
        lo, hi = plan.turns[c]
        place(lo, hi)
        if c >= 2:
            each_peer(spread_copy, c - 2, "wait_send")

        @pl.loop(0, n, unroll=2)
        def _(k):
            for i in range(lo, hi):
                problem = tab[i * n + k]
                block = tab[slots + i * n + k]
                for rank in range(ranks):
                    r["send1"][c % 2, k, rank, i - lo] = r["kv"][
                        rank * problems + problem, :, block
                    ]

        each_peer(spread_copy, c, "start")
        for rank in range(ranks):
            r[f"stash{c}"][me * ranks + rank] = r["send1"][c % 2, me, rank, : hi - lo]

    def fetch(c):
        lo, hi = plan.turns[c]
        each_peer(spread_copy, c, "wait_recv")
        if c >= 2:
            each_peer(fetch_copy, c - 2, "wait_send")

        @pl.loop(0, n, unroll=2)
        def _(child):
            for i in range(lo, hi):
                problem = tab[i * n + me]
                for slot in range(ranks):
                    parent = reqs[child, 0, slot * problems + problem]
                    r["send2"][c % 2, child, slot, i - lo] = r[f"stash{c}"][parent, i - lo]

        each_peer(fetch_copy, c, "start")
        r[f"got{c}"][me] = r["send2"][c % 2, me, :, : hi - lo]

    def unpack(c):
        lo, hi = plan.turns[c]
        each_peer(fetch_copy, c, "wait_recv")

        @pl.loop(0, n)
        def _(k):
            for i in range(lo, hi):
                for slot in range(ranks):
                    for part, name in enumerate(("kbuf", "vbuf")):
                        r[name][slot, i * n + k] = r[f"got{c}"][k, slot, i - lo, part]

    group = min(4, heads)
    factor = math.log2(math.e) / math.sqrt(HEAD)
    nt = (((1,), (1,)), ((), ()))

    def attend(c):
        first, last = plan.chunks[c]
        span = plan.most[last - 1]

        @pl.loop(0, (last - first) * ranks)
        def _(e):
            j = first + e // ranks
            slot = e % ranks
            beam = slot * problems + tab[at_order + j]
            start = tab[at_off + j]
            live = tab[at_len + j]
            keys, values = (
                jnp.concatenate([r[name][slot, start + i] for i in range(span // BLK)], axis=0)
                for name in ("kbuf", "vbuf")
            )
            new_keys, new_values = r["fresh"][beam, 0], r["fresh"][beam, 1]
            values = jnp.concatenate([values, jnp.ones_like(values)], axis=1)
            new_values = jnp.concatenate([new_values, jnp.ones_like(new_values)], axis=1)
            query = r["q"][beam]
            place = pl.multiple_of(e * step, step)
            for g in range(0, heads, group):
                part = jnp.concatenate(
                    [query[:, (g + h) * HEAD : (g + h + 1) * HEAD] for h in range(group)], axis=0
                )
                old = lax.dot_general(part, keys, nt, preferred_element_type=F32)
                new = lax.dot_general(part, new_keys, nt, preferred_element_type=F32)
                where = lax.broadcasted_iota(jnp.int32, old.shape, 1)
                old = jnp.where(where < live, old, -1e30)
                token = lax.broadcasted_iota(jnp.int32, new.shape, 0) % step
                other = lax.broadcasted_iota(jnp.int32, new.shape, 1)
                new = jnp.where(other <= token, new, -1e30)
                top = jnp.maximum(
                    jnp.max(old, axis=1, keepdims=True), jnp.max(new, axis=1, keepdims=True)
                )
                old = jnp.exp2((old - top) * factor).astype(BF16)
                new = jnp.exp2((new - top) * factor).astype(BF16)
                out = jnp.dot(old, values, preferred_element_type=F32)
                out = out + jnp.dot(new, new_values, preferred_element_type=F32)
                out = (out[:, :HEAD] / out[:, HEAD:]).astype(BF16)
                for h in range(group):
                    r["mixed"][pl.ds(place, step), (g + h) * HEAD : (g + h + 1) * HEAD] = out[
                        h * step : (h + 1) * step
                    ]

    def rows_of(c):
        first, last = plan.chunks[c]
        return (last - first) * ranks * step

    def project(c, block, target):
        rows = rows_of(c)
        column = pl.multiple_of(block * width, width)
        value = jnp.dot(
            r["mixed"][:rows, :], r["wt"][:, pl.ds(column, width)], preferred_element_type=F32
        )
        target[:rows, :] = value.astype(BF16)

    pending = {}

    def core_copy(c, hop):
        rows = rows_of(c)
        return pltpu.make_async_remote_copy(
            src_ref=r["csend"].at[hop, pl.ds(0, rows)],
            dst_ref=r["crecv"].at[c % 2, hop, pl.ds(0, rows)],
            send_sem=r["c_s"].at[hop],
            recv_sem=r["c_r"].at[c, hop],
            device_id=(me, my_z * 2 + 1 - my_core),
            device_id_type=MESH,
        )

    def block_for(c, hop):
        if c >= 1:
            pending["core", c - 1, hop].wait_send()
        project(c, chip_at(hop) * 2 + 1 - my_core, r["csend"].at[hop])
        pending["core", c, hop] = core_copy(c, hop)
        pending["core", c, hop].start()
        project(c, chip_at(hop) * 2 + my_core, r["own"].at[c % 2, hop])

    opposite = zs // 2
    ways = (1, zs - 1)
    piece = 64

    def z_copy(c, kind, way):
        half = rows_of(c) // 2
        low = (way if kind == "d" else 1 - way) * half
        if kind == "t":
            dst = r[f"trecv{c}"].at[way]
        else:
            dst = r[f"drecv{c}"].at[way, pl.ds(low, half)]
        return pltpu.make_async_remote_copy(
            src_ref=r[kind + "send"].at[way, pl.ds(0, half)],
            dst_ref=dst,
            send_sem=r[kind + "_s"].at[way],
            recv_sem=r[kind + "_r"].at[c, way],
            device_id=(me, chip_at(ways[way]) * 2 + my_core),
            device_id_type=MESH,
        )

    def send_z(c, kind, way):
        if c >= 1:
            pending[kind, c - 1, way].wait_send()
        half = rows_of(c) // 2
        hop = opposite if kind == "t" else ways[way]
        base = (1 - way) * half if kind == "n" else way * half

        @pl.loop(0, half // piece)
        def _(i):
            near = pl.ds(pl.multiple_of(i * piece, piece), piece)
            at = pl.ds(pl.multiple_of(base + i * piece, piece), piece)
            value = r["own"][c % 2, hop, at, :].astype(F32)
            value = value + r["crecv"][c % 2, hop, at, :].astype(F32)
            if kind == "d":
                value = value + r[f"trecv{c}"][way, near, :].astype(F32)
            r[kind + "send"][way, near, :] = value.astype(BF16)

        pending[kind, c, way] = z_copy(c, kind, way)
        pending[kind, c, way].start()

    def send_through(c):
        for way in range(2):
            pending["t", c, way].wait_recv()
            send_z(c, "d", way)

    def square_copy(c, hop):
        return pltpu.make_async_remote_copy(
            src_ref=r[f"sq{c}"],
            dst_ref=r[f"sqr{c}"].at[mine],
            send_sem=r["s_s"].at[c, hop],
            recv_sem=r["s_r"].at[c, hop],
            device_id=(me, tensor_peer(hop)),
            device_id_type=MESH,
        )

    def finish(c):
        first, last = plan.chunks[c]
        pending["core", c, 0].wait_recv()
        for way in range(2):
            pending["n", c, way].wait_recv()
            pending["d", c, way].wait_recv()

        @pl.loop(0, (last - first) * ranks)
        def _(e):
            j = first + e // ranks
            slot = e % ranks
            beam = slot * problems + tab[at_order + j]
            for low in range(0, step, 32):
                at = pl.ds(pl.multiple_of(e * step + low, 32), 32)
                value = r["own"][c % 2, 0, at, :].astype(F32)
                value = value + r["crecv"][c % 2, 0, at, :].astype(F32)
                value = value + r[f"drecv{c}"][0, at, :].astype(F32)
                value = value + r[f"drecv{c}"][1, at, :].astype(F32)
                value = value + r["res"][beam, low : low + 32, :].astype(F32)
                place = pl.ds(pl.multiple_of(slot * step + low, 32), 32)
                r["att"][j, place, :] = value
                value = value * value
                total = value[:, :LANES]
                for k in range(LANES, width, LANES):
                    total = total + value[:, k : k + LANES]
                r["sums"][e // ranks, place, :] = total

        for k in range(last - first):
            line = jnp.sum(r["sums"][k].T, axis=0, keepdims=True)
            r[f"sq{c}"][k] = jnp.broadcast_to(line, (8, line.shape[1]))
        r[f"sqr{c}"][mine] = r[f"sq{c}"][...]

        @pl.loop(1, tensor)
        def _(hop):
            square_copy(c, hop).start()

        if c + 2 < count:
            pl.semaphore_signal(
                r["credit"],
                inc=1,
                device_id=(me, my_z * 2 + 1 - my_core),
                device_id_type=MESH,
            )

    def project_all(c):
        if c >= 2:
            pl.semaphore_wait(r["credit"], 1)
        block_for(c, opposite)
        block_for(c, ways[0])
        pending["core", c, opposite].wait_recv()
        for way in range(2):
            send_z(c, "t", way)
        for way, hop in enumerate((ways[1], 0)):
            block_for(c, hop)
            pending["core", c, ways[way]].wait_recv()
            send_z(c, "n", way)

    loads["kv"].wait()
    loads["q"].start()
    loads["fresh"].start()
    spread(0)
    loads["wt"].start()
    loads["res"].start()
    if count > 1:
        spread(1)

    @pl.loop(1, n)
    def _(index):
        request_copy(index).wait_recv()

    table = pltpu.make_async_copy(r["reqv"], reqs, r["table_sem"])
    table.start()

    @pl.loop(0, plan.rows // BLK)
    def _(i):
        for name in ("kbuf", "vbuf"):
            for slot in range(ranks):
                r[name][slot, i] = jnp.zeros((BLK, HEAD), BF16)

    table.wait()
    fetch(0)
    if count > 2:
        spread(2)

    for c in range(count):
        if c + 1 < count:
            fetch(c + 1)
        if c + 3 < count:
            spread(c + 3)
        if c >= 1:
            send_through(c - 1)
        unpack(c)
        if c == 0:
            loads["q"].wait()
            loads["fresh"].wait()
        attend(c)
        if c == 0:
            loads["wt"].wait()
            loads["res"].wait()
        project_all(c)
        if c >= 1:
            finish(c - 1)
    send_through(count - 1)
    finish(count - 1)

    for c, (first, last) in enumerate(plan.chunks):

        @pl.loop(1, tensor)
        def _(hop):
            square_copy(c, hop).wait_recv()

        for k in range(last - first):
            line = r[f"sqr{c}"][0, k]
            for t in range(1, tensor):
                line = line + r[f"sqr{c}"][t, k]
            line = lax.rsqrt(line / plan.model + EPS)
            wide = jnp.broadcast_to(line[0:1, :], (LANES, line.shape[1]))
            r["scale"][first + k] = wide.T

    def out_copy(problem, slot):
        beam = slot * problems + problem
        return pltpu.make_async_copy(
            r["res"].at[beam], r["out_h"].at[beam], r["out_sem"].at[beam]
        )

    @pl.loop(0, problems)
    def _(problem):
        j = tab[at_rank + problem]
        for slot in range(ranks):
            for low in range(0, step, 32):
                at = slice(slot * step + low, slot * step + low + 32)
                scale = r["scale"][j, at, :]
                for k in range(0, width, LANES):
                    value = r["att"][j, at, k : k + LANES] * scale
                    value = value * r["gain"][k : k + LANES].astype(F32).reshape(1, LANES)
                    r["res"][slot * problems + problem, low : low + 32, k : k + LANES] = (
                        value.astype(BF16)
                    )
            out_copy(problem, slot).start()

    @pl.loop(0, problems)
    def _(problem):
        for slot in range(ranks):
            out_copy(problem, slot).wait()

    @pl.loop(1, n)
    def _(index):
        request_copy(index).wait_send()

    for c in range(max(0, count - 2), count):
        each_peer(spread_copy, c, "wait_send")
        each_peer(fetch_copy, c, "wait_send")
    for hop in range(zs):
        pending["core", count - 1, hop].wait_send()
    for way in range(2):
        for kind in "tnd":
            pending[kind, count - 1, way].wait_send()
    for c in range(count):

        @pl.loop(1, tensor)
        def _(hop):
            square_copy(c, hop).wait_send()


def on_device(
    queries, fresh_kv, kv_cache, parent_device, parent_rank, cache_length, out_weight, residual,
    norm_gain,
):
    n, tensor = lax.axis_size("dp"), lax.axis_size("tensor")
    beams, step, width = queries.shape
    ctx = kv_cache.shape[2]
    plan = Plan(n, tensor, beams, step, ctx, width, cache_length.shape[0], width * tensor)
    count, ranks, most = len(plan.chunks), plan.ranks, plan.row_most
    blocks = kv_cache.reshape(beams, 2, plan.blocks, BLK, HEAD)

    smem = pl.BlockSpec(memory_space=pltpu.SMEM)
    vmem = pl.BlockSpec(memory_space=pltpu.VMEM)
    hbm = pl.BlockSpec(memory_space=pl.ANY)
    inputs = [
        ("length", cache_length, smem),
        ("device", parent_device.reshape(beams), smem),
        ("rank", parent_rank, smem),
        ("gain", norm_gain, vmem),
        ("q_h", queries, hbm),
        ("fresh_h", fresh_kv, hbm),
        ("kv_h", blocks, hbm),
        ("wt_h", out_weight, hbm),
        ("res_h", residual, hbm),
    ]
    dma = lambda *shape: pltpu.SemaphoreType.DMA(shape)
    scratch = [
        ("q", pltpu.VMEM(queries.shape, BF16)),
        ("fresh", pltpu.VMEM(fresh_kv.shape, BF16)),
        ("kv", pltpu.VMEM(blocks.shape, BF16)),
        ("wt", pltpu.VMEM(out_weight.shape, BF16)),
        ("res", pltpu.VMEM(residual.shape, BF16)),
        ("kbuf", pltpu.VMEM((ranks, plan.rows // BLK, BLK, HEAD), BF16)),
        ("vbuf", pltpu.VMEM((ranks, plan.rows // BLK, BLK, HEAD), BF16)),
        ("send1", pltpu.VMEM((2, n, ranks, plan.turn_most, 2, BLK, HEAD), BF16)),
        ("send2", pltpu.VMEM((2, n, ranks, plan.turn_most, 2, BLK, HEAD), BF16)),
        ("tab", pltpu.SMEM((2 * plan.slots + 4 * plan.problems,), jnp.int32)),
        ("req", pltpu.VMEM((8, LANES), jnp.int32)),
        ("reqv", pltpu.VMEM((n, 8, LANES), jnp.int32)),
        ("reqs", pltpu.SMEM((n, 8, LANES), jnp.int32)),
        ("mixed", pltpu.VMEM((most, width), BF16)),
        ("own", pltpu.VMEM((2, plan.zs, most, width), BF16)),
        ("csend", pltpu.VMEM((plan.zs, most, width), BF16)),
        ("crecv", pltpu.VMEM((2, plan.zs, most, width), BF16)),
        ("tsend", pltpu.VMEM((2, most // 2, width), BF16)),
        ("nsend", pltpu.VMEM((2, most // 2, width), BF16)),
        ("dsend", pltpu.VMEM((2, most // 2, width), BF16)),
        ("att", pltpu.VMEM((plan.problems, ranks * step, width), F32)),
        ("sums", pltpu.VMEM((most // (ranks * step), ranks * step, LANES), F32)),
        ("scale", pltpu.VMEM((plan.problems, ranks * step, LANES), F32)),
        ("load_sem", dma(5)),
        ("table_sem", pltpu.SemaphoreType.DMA),
        ("rq_s", dma(n)),
        ("rq_r", dma(n)),
        ("p1_s", dma(count, n)),
        ("p1_r", dma(count, n)),
        ("p2_s", dma(count, n)),
        ("p2_r", dma(count, n)),
        ("c_s", dma(plan.zs)),
        ("c_r", dma(count, plan.zs)),
        ("t_s", dma(2)),
        ("t_r", dma(count, 2)),
        ("n_s", dma(2)),
        ("n_r", dma(count, 2)),
        ("d_s", dma(2)),
        ("d_r", dma(count, 2)),
        ("s_s", dma(count, tensor)),
        ("s_r", dma(count, tensor)),
        ("out_sem", dma(beams)),
        ("credit", pltpu.SemaphoreType.REGULAR),
    ]
    for c in range(count):
        (first, last), (lo, hi) = plan.chunks[c], plan.turns[c]
        rows = (last - first) * ranks * step
        scratch += [
            (f"stash{c}", pltpu.VMEM((n * ranks, hi - lo, 2, BLK, HEAD), BF16)),
            (f"got{c}", pltpu.VMEM((n, ranks, hi - lo, 2, BLK, HEAD), BF16)),
            (f"trecv{c}", pltpu.VMEM((2, rows // 2, width), BF16)),
            (f"drecv{c}", pltpu.VMEM((2, rows, width), BF16)),
            (f"sq{c}", pltpu.VMEM((last - first, 8, ranks * step), F32)),
            (f"sqr{c}", pltpu.VMEM((tensor, last - first, 8, ranks * step), F32)),
        ]
    names = [i[0] for i in inputs] + ["out_h"] + [s[0] for s in scratch]
    rows = beams * step
    return pl.pallas_call(
        functools.partial(kernel, plan, names),
        out_shape=jax.ShapeDtypeStruct(residual.shape, BF16),
        in_specs=[i[2] for i in inputs],
        out_specs=hbm,
        scratch_shapes=[s[1] for s in scratch],
        compiler_params=pltpu.CompilerParams(
            collective_id=0, has_side_effects=True, vmem_limit_bytes=64 * 1024 * 1024 - 4096
        ),
        cost_estimate=pl.CostEstimate(
            flops=2 * rows * width * width * tensor + 4 * rows * width * (ctx + step),
            bytes_accessed=30 * 1024 * 1024,
            transcendentals=rows * (width // HEAD) * (ctx + step),
        ),
        name="step_scoring",
    )(*[i[1] for i in inputs])


def solution(mesh):
    placed = (
        P("dp", None, "tensor"),
        P("dp", None, None, "tensor"),
        P("dp", None, None, "tensor"),
        P("dp", None),
        P("dp"),
        P(),
        P("tensor", None),
        P("dp", None, "tensor"),
        P("tensor"),
    )
    return jax.shard_map(
        on_device, mesh=mesh, in_specs=placed, out_specs=P("dp", None, "tensor"), check_vma=False
    )
```

```python
import functools
import math

import jax
import jax.numpy as jnp
from jax import lax
from jax.experimental import pallas as pl
from jax.experimental.pallas import tpu as pltpu
from jax.sharding import PartitionSpec as P

MESH = pl.DeviceIdType.MESH
HEAD = 128
BLK = 16
LANES = 128
EPS = 1e-06
F32 = jnp.float32
BF16 = jnp.bfloat16
STRIDE = 7
MIX = (1, 4, 3, 12, 6, 9, 14, 11, 5, 15, 7, 13, 10, 2, 8)


class Plan:
    def __init__(self, n, tensor, beams, step, ctx, width, problems, model):
        self.n, self.tensor, self.zs = n, tensor, tensor // 2
        self.beams, self.step, self.ctx, self.width = beams, step, ctx, width
        self.problems, self.ranks, self.model = problems, beams // problems, model
        self.side = math.isqrt(n)
        total = problems * ctx * 5 // 8
        rest = total - ctx
        before = [
            (rest * j // (problems - 1) + (BLK - 1) * j) // BLK for j in range(problems)
        ]
        before.append(ctx // BLK + before[problems - 1])
        ends = [1, 3, 5, 7, 8] if problems == 8 else list(range(1, problems + 1))
        self.chunks, self.turns = [], []
        low, turn = 0, 0
        for end in ends:
            last = -(-before[end] // n)
            self.chunks.append((low, end))
            self.turns.append((turn, last))
            low, turn = end, last
        self.slots = turn * n
        self.blocks = ctx // BLK
        self.most = []
        for j in range(problems):
            bound = rest // (problems - 1 - j) if j < problems - 1 else ctx
            self.most.append(min(ctx, -(-bound // LANES) * LANES))
        self.rows = max(
            [self.slots * BLK] + [before[j] * BLK + self.most[j] for j in range(problems)]
        )
        self.rows = -(-self.rows // BLK) * BLK
        self.row_most = max(e - s for s, e in self.chunks) * self.ranks * step
        self.turn_most = max(e - s for s, e in self.turns)


def kernel(plan, names, *refs):
    r = dict(zip(names, refs))
    n, zs, tensor = plan.n, plan.zs, plan.tensor
    ranks, problems, step, width = plan.ranks, plan.problems, plan.step, plan.width
    heads = width // HEAD
    side = plan.side
    count = len(plan.chunks)
    slots = plan.slots
    me = lax.axis_index("dp")
    mine = lax.axis_index("tensor")

    def div(a, b):
        return lax.div(a, jnp.int32(b))

    def rem(a, b):
        return lax.rem(a, jnp.int32(b))

    my_y, my_x = div(me, side), rem(me, side)
    my_z, my_core = div(mine, 2), rem(mine, 2)
    tab, reqs = r["tab"], r["reqs"]
    at_order, at_off, at_len, at_rank = (2 * slots + problems * i for i in range(4))

    def plane_peer(index):
        if isinstance(index, int):
            hop = MIX[index - 1] if n == 16 else index
            return hop, rem(my_y + hop // side, side) * side + rem(my_x + hop % side, side)
        hop = rem(index * STRIDE, n)
        there = rem(my_y + div(hop, side), side) * side + rem(my_x + rem(hop, side), side)
        return hop, there

    def tensor_peer(hop):
        return rem(mine + hop, tensor)

    def chip_at(hop):
        return rem(my_z + hop, zs)

    barrier = pltpu.get_barrier_semaphore()

    @pl.loop(1, n)
    def _(index):
        hop, there = plane_peer(index)
        pl.semaphore_signal(barrier, inc=1, device_id=(there, mine), device_id_type=MESH)

    @pl.loop(1, tensor)
    def _(hop):
        pl.semaphore_signal(
            barrier, inc=1, device_id=(me, tensor_peer(hop)), device_id_type=MESH
        )

    loads = {}
    for i, name in enumerate(("kv", "q", "fresh", "wt", "res")):
        loads[name] = pltpu.make_async_copy(r[name + "_h"], r[name], r["load_sem"].at[i])
    loads["kv"].start()

    lengths = [r["length"][p] for p in range(problems)]
    rank_of = []
    for p in range(problems):
        found = jnp.int32(0)
        for o in range(problems):
            if o != p:
                ahead = lengths[o] <= lengths[p] if o < p else lengths[o] < lengths[p]
                found = found + jnp.where(ahead, 1, 0)
        rank_of.append(found)
        tab[at_rank + p] = found
    starts = []
    for j in range(problems):
        which, long, start = jnp.int32(0), jnp.int32(0), jnp.int32(0)
        for p in range(problems):
            hit = rank_of[p] == j
            which = which + jnp.where(hit, p, 0)
            long = long + jnp.where(hit, lengths[p], 0)
            used = lax.div(lengths[p] + (BLK - 1), jnp.int32(BLK))
            start = start + jnp.where(rank_of[p] < j, used, 0)
        tab[at_order + j], tab[at_len + j], tab[at_off + j] = which, long, start
        starts.append(start)

    def place(lo, hi):
        @pl.loop(lo * n, hi * n, unroll=4)
        def _(slot):
            turn = jnp.int32(0)
            for j in range(1, problems):
                turn = turn + jnp.where(starts[j] <= slot, 1, 0)
            tab[slot] = tab[at_order + turn]
            block = slot - tab[at_off + turn]
            tab[slots + slot] = jnp.minimum(jnp.maximum(block, 0), plan.blocks - 1)

    lane = lax.broadcasted_iota(jnp.int32, (8, LANES), 1)
    wanted = jnp.zeros((8, LANES), jnp.int32)
    for b in range(plan.beams):
        value = r["device"][b] * ranks + r["rank"][b]
        wanted = jnp.where(lane == b, value, wanted)
    r["req"][...] = wanted

    def request_copy(index):
        hop, there = plane_peer(index)
        return pltpu.make_async_remote_copy(
            src_ref=r["req"],
            dst_ref=r["reqv"].at[me],
            send_sem=r["rq_s"].at[hop],
            recv_sem=r["rq_r"].at[hop],
            device_id=(there, mine),
            device_id_type=MESH,
        )

    r["reqv"][me] = r["req"][...]

    def spread_copy(c, index):
        hop, there = plane_peer(index)
        lo, hi = plan.turns[c]
        return pltpu.make_async_remote_copy(
            src_ref=r["send1"].at[c % 2, there, pl.ds(0, ranks * (hi - lo))],
            dst_ref=r[f"stash{c}"].at[pl.ds(me * (ranks * (hi - lo)), ranks * (hi - lo))],
            send_sem=r["p1_s"].at[c, hop],
            recv_sem=r["p1_r"].at[c, hop],
            device_id=(there, mine),
            device_id_type=MESH,
        )

    def fetch_copy(c, index):
        hop, there = plane_peer(index)
        lo, hi = plan.turns[c]
        return pltpu.make_async_remote_copy(
            src_ref=r["send2"].at[c % 2, there, pl.ds(0, ranks * (hi - lo))],
            dst_ref=r[f"got{c}"].at[me],
            send_sem=r["p2_s"].at[c, hop],
            recv_sem=r["p2_r"].at[c, hop],
            device_id=(there, mine),
            device_id_type=MESH,
        )

    def each_peer(make, c, what):
        for index in range(1, n):
            getattr(make(c, index), what)()

    def pack(c):
        lo, hi = plan.turns[c]
        place(lo, hi)
        if c >= 2:
            each_peer(spread_copy, c - 2, "wait_send")

        @pl.loop(0, n, unroll=2)
        def _(k):
            for i in range(lo, hi):
                problem = tab[i * n + k]
                block = tab[slots + i * n + k]
                for rank in range(ranks):
                    r["send1"][c % 2, k, rank * (hi - lo) + i - lo] = r["kv"][
                        rank * problems + problem, :, block
                    ]

    def spread(c):
        lo, hi = plan.turns[c]
        each_peer(spread_copy, c, "start")
        for k in range(ranks * (hi - lo)):
            r[f"stash{c}"][me * (ranks * (hi - lo)) + k] = r["send1"][c % 2, me, k]

    def fetch(c):
        lo, hi = plan.turns[c]
        each_peer(spread_copy, c, "wait_recv")
        if c >= 2:
            each_peer(fetch_copy, c - 2, "wait_send")

        @pl.loop(0, n, unroll=2)
        def _(child):
            for i in range(lo, hi):
                problem = tab[i * n + me]
                for slot in range(ranks):
                    parent = reqs[child, 0, slot * problems + problem]
                    r["send2"][c % 2, child, slot * (hi - lo) + i - lo] = r[f"stash{c}"][
                        parent * (hi - lo) + i - lo
                    ]

        each_peer(fetch_copy, c, "start")
        r[f"got{c}"][me] = r["send2"][c % 2, me, : ranks * (hi - lo)]

    def unpack(c):
        lo, hi = plan.turns[c]
        each_peer(fetch_copy, c, "wait_recv")

        @pl.loop(0, n)
        def _(k):
            for i in range(lo, hi):
                for slot in range(ranks):
                    for part, name in enumerate(("kbuf", "vbuf")):
                        r[name][slot, i * n + k] = r[f"got{c}"][
                            k, slot * (hi - lo) + i - lo, part
                        ]

    group = min(4, heads)
    factor = math.log2(math.e) / math.sqrt(HEAD)
    nt = (((1,), (1,)), ((), ()))

    def attend(c):
        first, last = plan.chunks[c]
        span = plan.most[last - 1]

        @pl.loop(0, (last - first) * ranks)
        def _(e):
            j = first + e // ranks
            slot = e % ranks
            beam = slot * problems + tab[at_order + j]
            start = tab[at_off + j]
            live = tab[at_len + j]
            keys, values = (
                jnp.concatenate([r[name][slot, start + i] for i in range(span // BLK)], axis=0)
                for name in ("kbuf", "vbuf")
            )
            new_keys, new_values = r["fresh"][beam, 0], r["fresh"][beam, 1]
            values = jnp.concatenate([values, jnp.ones_like(values)], axis=1)
            new_values = jnp.concatenate([new_values, jnp.ones_like(new_values)], axis=1)
            query = r["q"][beam]
            place = pl.multiple_of(e * step, step)
            for g in range(0, heads, group):
                part = jnp.concatenate(
                    [query[:, (g + h) * HEAD : (g + h + 1) * HEAD] for h in range(group)], axis=0
                )
                old = lax.dot_general(part, keys, nt, preferred_element_type=F32)
                new = lax.dot_general(part, new_keys, nt, preferred_element_type=F32)
                where = lax.broadcasted_iota(jnp.int32, old.shape, 1)
                old = jnp.where(where < live, old, -1e30)
                token = lax.broadcasted_iota(jnp.int32, new.shape, 0) % step
                other = lax.broadcasted_iota(jnp.int32, new.shape, 1)
                new = jnp.where(other <= token, new, -1e30)
                top = jnp.maximum(
                    jnp.max(old, axis=1, keepdims=True), jnp.max(new, axis=1, keepdims=True)
                )
                old = jnp.exp2((old - top) * factor).astype(BF16)
                new = jnp.exp2((new - top) * factor).astype(BF16)
                out = jnp.dot(old, values, preferred_element_type=F32)
                out = out + jnp.dot(new, new_values, preferred_element_type=F32)
                out = (out[:, :HEAD] / out[:, HEAD:]).astype(BF16)
                for h in range(group):
                    r["mixed"][pl.ds(place, step), (g + h) * HEAD : (g + h + 1) * HEAD] = out[
                        h * step : (h + 1) * step
                    ]

    def rows_of(c):
        first, last = plan.chunks[c]
        return (last - first) * ranks * step

    def project(c, block, target):
        rows = rows_of(c)
        column = pl.multiple_of(block * width, width)
        value = jnp.dot(
            r["mixed"][:rows, :], r["wt"][:, pl.ds(column, width)], preferred_element_type=F32
        )
        target[:rows, :] = value.astype(BF16)

    pending = {}

    def core_copy(c, hop):
        rows = rows_of(c)
        return pltpu.make_async_remote_copy(
            src_ref=r["csend"].at[hop, pl.ds(0, rows)],
            dst_ref=r["crecv"].at[c % 2, hop, pl.ds(0, rows)],
            send_sem=r["c_s"].at[hop],
            recv_sem=r["c_r"].at[c, hop],
            device_id=(me, my_z * 2 + 1 - my_core),
            device_id_type=MESH,
        )

    def block_for(c, hop):
        if c >= 1:
            pending["core", c - 1, hop].wait_send()
        project(c, chip_at(hop) * 2 + 1 - my_core, r["csend"].at[hop])
        pending["core", c, hop] = core_copy(c, hop)
        pending["core", c, hop].start()
        project(c, chip_at(hop) * 2 + my_core, r["own"].at[c % 2, hop])

    opposite = zs // 2
    ways = (1, zs - 1)
    piece = 64

    def z_copy(c, kind, way):
        half = rows_of(c) // 2
        low = (way if kind == "d" else 1 - way) * half
        if kind == "t":
            dst = r[f"trecv{c}"].at[way]
        else:
            dst = r[f"drecv{c}"].at[way, pl.ds(low, half)]
        return pltpu.make_async_remote_copy(
            src_ref=r[kind + "send"].at[way, pl.ds(0, half)],
            dst_ref=dst,
            send_sem=r[kind + "_s"].at[way],
            recv_sem=r[kind + "_r"].at[c, way],
            device_id=(me, chip_at(ways[way]) * 2 + my_core),
            device_id_type=MESH,
        )

    def send_z(c, kind, way):
        if c >= 1:
            pending[kind, c - 1, way].wait_send()
        half = rows_of(c) // 2
        hop = opposite if kind == "t" else ways[way]
        base = (1 - way) * half if kind == "n" else way * half

        @pl.loop(0, half // piece)
        def _(i):
            near = pl.ds(pl.multiple_of(i * piece, piece), piece)
            at = pl.ds(pl.multiple_of(base + i * piece, piece), piece)
            value = r["own"][c % 2, hop, at, :].astype(F32)
            value = value + r["crecv"][c % 2, hop, at, :].astype(F32)
            if kind == "d":
                value = value + r[f"trecv{c}"][way, near, :].astype(F32)
            r[kind + "send"][way, near, :] = value.astype(BF16)

        pending[kind, c, way] = z_copy(c, kind, way)
        pending[kind, c, way].start()

    def send_through(c):
        for way in range(2):
            pending["t", c, way].wait_recv()
            send_z(c, "d", way)

    def square_copy(c, hop):
        return pltpu.make_async_remote_copy(
            src_ref=r[f"sq{c}"],
            dst_ref=r[f"sqr{c}"].at[mine],
            send_sem=r["s_s"].at[c, hop],
            recv_sem=r["s_r"].at[c, hop],
            device_id=(me, tensor_peer(hop)),
            device_id_type=MESH,
        )

    def finish(c):
        first, last = plan.chunks[c]
        pending["core", c, 0].wait_recv()
        for way in range(2):
            pending["n", c, way].wait_recv()
            pending["d", c, way].wait_recv()

        @pl.loop(0, (last - first) * ranks)
        def _(e):
            j = first + e // ranks
            slot = e % ranks
            beam = slot * problems + tab[at_order + j]
            for low in range(0, step, 32):
                at = pl.ds(pl.multiple_of(e * step + low, 32), 32)
                value = r["own"][c % 2, 0, at, :].astype(F32)
                value = value + r["crecv"][c % 2, 0, at, :].astype(F32)
                value = value + r[f"drecv{c}"][0, at, :].astype(F32)
                value = value + r[f"drecv{c}"][1, at, :].astype(F32)
                value = value + r["res"][beam, low : low + 32, :].astype(F32)
                place = pl.ds(pl.multiple_of(slot * step + low, 32), 32)
                r["att"][j, place, :] = value
                value = value * value
                total = value[:, :LANES]
                for k in range(LANES, width, LANES):
                    total = total + value[:, k : k + LANES]
                r["sums"][e // ranks, place, :] = total

        for k in range(last - first):
            line = jnp.sum(r["sums"][k].T, axis=0, keepdims=True)
            r[f"sq{c}"][k] = jnp.broadcast_to(line, (8, line.shape[1]))
        r[f"sqr{c}"][mine] = r[f"sq{c}"][...]

        @pl.loop(1, tensor)
        def _(hop):
            square_copy(c, hop).start()

        if c + 2 < count:
            pl.semaphore_signal(
                r["credit"],
                inc=1,
                device_id=(me, my_z * 2 + 1 - my_core),
                device_id_type=MESH,
            )

    def project_all(c):
        if c >= 2:
            pl.semaphore_wait(r["credit"], 1)
        block_for(c, opposite)
        block_for(c, ways[0])
        pending["core", c, opposite].wait_recv()
        for way in range(2):
            send_z(c, "t", way)
        for way, hop in enumerate((ways[1], 0)):
            block_for(c, hop)
            pending["core", c, ways[way]].wait_recv()
            send_z(c, "n", way)

    loads["kv"].wait()
    loads["q"].start()
    loads["fresh"].start()
    pack(0)
    pl.semaphore_wait(barrier, n - 1 + tensor - 1)
    spread(0)

    @pl.loop(1, n)
    def _(index):
        request_copy(index).start()

    loads["wt"].start()
    loads["res"].start()
    if count > 1:
        pack(1)
        spread(1)

    @pl.loop(1, n)
    def _(index):
        request_copy(index).wait_recv()

    table = pltpu.make_async_copy(r["reqv"], reqs, r["table_sem"])
    table.start()

    @pl.loop(0, plan.rows // BLK)
    def _(i):
        for name in ("kbuf", "vbuf"):
            for slot in range(ranks):
                r[name][slot, i] = jnp.zeros((BLK, HEAD), BF16)

    table.wait()
    fetch(0)
    if count > 2:
        pack(2)
        spread(2)

    for c in range(count):
        if c + 1 < count:
            fetch(c + 1)
        if c + 3 < count:
            pack(c + 3)
            spread(c + 3)
        if c >= 1:
            send_through(c - 1)
        unpack(c)
        if c == 0:
            loads["q"].wait()
            loads["fresh"].wait()
        attend(c)
        if c == 0:
            loads["wt"].wait()
            loads["res"].wait()
        project_all(c)
        if c >= 1:
            finish(c - 1)
    send_through(count - 1)
    finish(count - 1)

    for c, (first, last) in enumerate(plan.chunks):

        @pl.loop(1, tensor)
        def _(hop):
            square_copy(c, hop).wait_recv()

        for k in range(last - first):
            line = r[f"sqr{c}"][0, k]
            for t in range(1, tensor):
                line = line + r[f"sqr{c}"][t, k]
            line = lax.rsqrt(line / plan.model + EPS)
            wide = jnp.broadcast_to(line[0:1, :], (LANES, line.shape[1]))
            r["scale"][first + k] = wide.T

    def out_copy(problem, slot):
        beam = slot * problems + problem
        return pltpu.make_async_copy(
            r["res"].at[beam], r["out_h"].at[beam], r["out_sem"].at[beam]
        )

    @pl.loop(0, problems)
    def _(problem):
        j = tab[at_rank + problem]
        for slot in range(ranks):
            for low in range(0, step, 32):
                at = slice(slot * step + low, slot * step + low + 32)
                scale = r["scale"][j, at, :]
                for k in range(0, width, LANES):
                    value = r["att"][j, at, k : k + LANES] * scale
                    value = value * r["gain"][k : k + LANES].astype(F32).reshape(1, LANES)
                    r["res"][slot * problems + problem, low : low + 32, k : k + LANES] = (
                        value.astype(BF16)
                    )
            out_copy(problem, slot).start()

    @pl.loop(0, problems)
    def _(problem):
        for slot in range(ranks):
            out_copy(problem, slot).wait()

    @pl.loop(1, n)
    def _(index):
        request_copy(index).wait_send()

    for c in range(max(0, count - 2), count):
        each_peer(spread_copy, c, "wait_send")
        each_peer(fetch_copy, c, "wait_send")
    for hop in range(zs):
        pending["core", count - 1, hop].wait_send()
    for way in range(2):
        for kind in "tnd":
            pending[kind, count - 1, way].wait_send()
    for c in range(count):

        @pl.loop(1, tensor)
        def _(hop):
            square_copy(c, hop).wait_send()


PIECES = 4


def hand_over(source, target, held, in_sem, out_sem):
    size = source.shape[0] // PIECES
    for i in range(PIECES):
        at = pl.ds(i * size, size)
        pltpu.make_async_copy(source.at[at], held.at[at], in_sem.at[i]).start()
    for i in range(PIECES):
        at = pl.ds(i * size, size)
        pltpu.make_async_copy(source.at[at], held.at[at], in_sem.at[i]).wait()
        pltpu.make_async_copy(held.at[at], target.at[at], out_sem.at[i]).start()
    for i in range(PIECES):
        at = pl.ds(i * size, size)
        pltpu.make_async_copy(held.at[at], target.at[at], out_sem.at[i]).wait()


def on_device(
    queries, fresh_kv, kv_cache, parent_device, parent_rank, cache_length, out_weight, residual,
    norm_gain,
):
    n, tensor = lax.axis_size("dp"), lax.axis_size("tensor")
    beams, step, width = queries.shape
    ctx = kv_cache.shape[2]
    plan = Plan(n, tensor, beams, step, ctx, width, cache_length.shape[0], width * tensor)
    count, ranks, most = len(plan.chunks), plan.ranks, plan.row_most
    blocks = kv_cache.reshape(beams, 2, plan.blocks, BLK, HEAD)

    smem = pl.BlockSpec(memory_space=pltpu.SMEM)
    vmem = pl.BlockSpec(memory_space=pltpu.VMEM)
    hbm = pl.BlockSpec(memory_space=pl.ANY)
    inputs = [
        ("length", cache_length, smem),
        ("device", parent_device.reshape(beams), smem),
        ("rank", parent_rank, smem),
        ("gain", norm_gain, vmem),
        ("q_h", queries, hbm),
        ("fresh_h", fresh_kv, hbm),
        ("kv_h", blocks, hbm),
        ("wt_h", out_weight, hbm),
        ("res_h", residual, hbm),
    ]
    dma = lambda *shape: pltpu.SemaphoreType.DMA(shape)
    scratch = [
        ("q", pltpu.VMEM(queries.shape, BF16)),
        ("fresh", pltpu.VMEM(fresh_kv.shape, BF16)),
        ("kv", pltpu.VMEM(blocks.shape, BF16)),
        ("wt", pltpu.VMEM(out_weight.shape, BF16)),
        ("res", pltpu.VMEM(residual.shape, BF16)),
        ("kbuf", pltpu.VMEM((ranks, plan.rows // BLK, BLK, HEAD), BF16)),
        ("vbuf", pltpu.VMEM((ranks, plan.rows // BLK, BLK, HEAD), BF16)),
        ("send1", pltpu.VMEM((2, n, ranks * plan.turn_most, 2, BLK, HEAD), BF16)),
        ("send2", pltpu.VMEM((2, n, ranks * plan.turn_most, 2, BLK, HEAD), BF16)),
        ("tab", pltpu.SMEM((2 * plan.slots + 4 * plan.problems,), jnp.int32)),
        ("req", pltpu.VMEM((8, LANES), jnp.int32)),
        ("reqv", pltpu.VMEM((n, 8, LANES), jnp.int32)),
        ("reqs", pltpu.SMEM((n, 8, LANES), jnp.int32)),
        ("mixed", pltpu.VMEM((most, width), BF16)),
        ("own", pltpu.VMEM((2, plan.zs, most, width), BF16)),
        ("csend", pltpu.VMEM((plan.zs, most, width), BF16)),
        ("crecv", pltpu.VMEM((2, plan.zs, most, width), BF16)),
        ("tsend", pltpu.VMEM((2, most // 2, width), BF16)),
        ("nsend", pltpu.VMEM((2, most // 2, width), BF16)),
        ("dsend", pltpu.VMEM((2, most // 2, width), BF16)),
        ("att", pltpu.VMEM((plan.problems, ranks * step, width), F32)),
        ("sums", pltpu.VMEM((most // (ranks * step), ranks * step, LANES), F32)),
        ("scale", pltpu.VMEM((plan.problems, ranks * step, LANES), F32)),
        ("load_sem", dma(5)),
        ("table_sem", pltpu.SemaphoreType.DMA),
        ("rq_s", dma(n)),
        ("rq_r", dma(n)),
        ("p1_s", dma(count, n)),
        ("p1_r", dma(count, n)),
        ("p2_s", dma(count, n)),
        ("p2_r", dma(count, n)),
        ("c_s", dma(plan.zs)),
        ("c_r", dma(count, plan.zs)),
        ("t_s", dma(2)),
        ("t_r", dma(count, 2)),
        ("n_s", dma(2)),
        ("n_r", dma(count, 2)),
        ("d_s", dma(2)),
        ("d_r", dma(count, 2)),
        ("s_s", dma(count, tensor)),
        ("s_r", dma(count, tensor)),
        ("out_sem", dma(beams)),
        ("credit", pltpu.SemaphoreType.REGULAR),
    ]
    for c in range(count):
        (first, last), (lo, hi) = plan.chunks[c], plan.turns[c]
        rows = (last - first) * ranks * step
        scratch += [
            (f"stash{c}", pltpu.VMEM((n * ranks * (hi - lo), 2, BLK, HEAD), BF16)),
            (f"got{c}", pltpu.VMEM((n, ranks * (hi - lo), 2, BLK, HEAD), BF16)),
            (f"trecv{c}", pltpu.VMEM((2, rows // 2, width), BF16)),
            (f"drecv{c}", pltpu.VMEM((2, rows, width), BF16)),
            (f"sq{c}", pltpu.VMEM((last - first, 8, ranks * step), F32)),
            (f"sqr{c}", pltpu.VMEM((tensor, last - first, 8, ranks * step), F32)),
        ]
    names = [i[0] for i in inputs] + ["out_h"] + [s[0] for s in scratch]
    rows = beams * step
    scored = pl.pallas_call(
        functools.partial(kernel, plan, names),
        out_shape=jax.ShapeDtypeStruct(residual.shape, BF16),
        in_specs=[i[2] for i in inputs],
        out_specs=hbm,
        scratch_shapes=[s[1] for s in scratch],
        compiler_params=pltpu.CompilerParams(
            collective_id=0, has_side_effects=True, vmem_limit_bytes=64 * 1024 * 1024 - 4096
        ),
        cost_estimate=pl.CostEstimate(
            flops=2 * rows * width * width * tensor + 4 * rows * width * (ctx + step),
            bytes_accessed=30 * 1024 * 1024,
            transcendentals=rows * (width // HEAD) * (ctx + step),
        ),
        name="step_scoring",
    )(*[i[1] for i in inputs])
    return pl.pallas_call(
        hand_over,
        out_shape=jax.ShapeDtypeStruct(residual.shape, BF16),
        in_specs=[hbm],
        out_specs=hbm,
        scratch_shapes=[
            pltpu.VMEM(residual.shape, BF16),
            pltpu.SemaphoreType.DMA((PIECES,)),
            pltpu.SemaphoreType.DMA((PIECES,)),
        ],
        name="hand_over",
    )(scored)


def solution(mesh):
    placed = (
        P("dp", None, "tensor"),
        P("dp", None, None, "tensor"),
        P("dp", None, None, "tensor"),
        P("dp", None),
        P("dp"),
        P(),
        P("tensor", None),
        P("dp", None, "tensor"),
        P("tensor"),
    )
    return jax.shard_map(
        on_device, mesh=mesh, in_specs=placed, out_specs=P("dp", None, "tensor"), check_vma=False
    )
```
